512 devices in a mesh: dp: 64 (over z, x_hi, core), layer: 8 (over x_lo, y).
Axes of the slice: x: 4 (x_hi: 2, x_lo: 2; x = x_hi * 2 + x_lo), y: 4, z: 16, core: 2. Of those that a mesh axis runs over, the one named last changes fastest.
Arguments:
- train_grads: bfloat16 [16384, 8, 4096], P('dp', 'layer'), may hold values from -6 to 6
- query_grads: bfloat16 [4, 512, 8, 4096], P(None, 'dp', 'layer'), may hold values from -6 to 6
- out_basis: float32 [8, 64, 64], P('layer'), may hold values from -0.75 to 0.75
- in_basis: float32 [8, 64, 64], P('layer'), may hold values from -0.75 to 0.75
- eigenvalues: float32 [8, 4096], P('layer'), may hold values from 0.5 to 8
- block_order: int32 [4], replicated, may hold values from 0 to 3, each once
Outputs:
- scores: float32 [3, 512, 16384], P(None, 'layer', 'dp')
The draws below stay inside these ranges and needn't reach their ends.
Inputs may be any that keep to these rules, and one draw needn't show every extreme that they name: `block_order`: a permutation of 0 to 3.
All inputs are finite; a program needn't handle non-finite values.
Results may differ from the reference program's by a relative error of at most 0.0029.
Values may be sent and summed in bfloat16 or wider, within the bound.
A program may use at most 64 MiB of HBM per device.

```python
import math
import jax
import jax.numpy as jnp
from jax import lax

FO = 64
FI = 64
PROJ = 4096
LAYERS = 8
TRAIN = 16384
QUERIES = 512
NBLK = 4
STEPS = 3


def level_of(rng, extent, cuts, smallest, high):
    level, own = 1.0, jax.random.fold_in(rng, 6)
    for position, parts in cuts:
        steps = jnp.exp(jax.random.uniform(jax.random.fold_in(own, position), (parts,), jnp.float32, smallest / len(cuts), high / len(cuts)))
        level = level * jnp.repeat(steps, extent[position] // parts).reshape([-1 if axis == position else 1 for axis in range(len(extent))])
    return level


def gaussian(key, shape, spread, bound, cuts=(), kind=jnp.bfloat16):
    array = jax.random.normal(key, shape, jnp.float32) * spread
    if len(cuts) > 0:
        array = level_of(key, shape, cuts, -0.22, 0.18) * array
    return jnp.clip(array, min=-bound, max=bound).astype(kind)


def setup_inputs(seed: int = 0) -> dict:
    splits = jax.random.split(jax.random.key(seed), 7)
    train_grads = gaussian(splits[0], (TRAIN, LAYERS, PROJ), 1.0, 6.0, ((0, 64), (1, 8)))
    query_grads = gaussian(splits[1], (NBLK, QUERIES, LAYERS, PROJ), 1.0, 6.0, ((1, 64), (2, 8)))
    out_basis = gaussian(splits[2], (LAYERS, FO, FO), FO ** -0.5, 0.75, ((0, 8),), jnp.float32)
    in_basis = gaussian(splits[3], (LAYERS, FI, FI), FI ** -0.5, 0.75, ((0, 8),), jnp.float32)
    eigenvalues = jnp.clip(jnp.exp(math.log(8.0) - 2.7725887 * jax.random.uniform(splits[4], (LAYERS, PROJ), jnp.float32) ** level_of(splits[4], (LAYERS, PROJ), ((0, 8),), -0.2, 0.2)), 0.5, 8.0)
    block_order = jax.random.permutation(splits[5], NBLK).astype(jnp.int32)
    return {"train_grads": train_grads, "query_grads": query_grads, "out_basis": out_basis, "in_basis": in_basis, "eigenvalues": eigenvalues, "block_order": block_order}


def precondition(raw_rows, out_basis, in_basis, eigenvalues):
    row_total = raw_rows.shape[0]
    layer_count = raw_rows.shape[1]
    proj_width = raw_rows.shape[2]
    out_width = out_basis.shape[1]
    in_width = in_basis.shape[1]
    precise = lax.Precision.HIGHEST
    grid_form = raw_rows.astype(jnp.float32).reshape(row_total, layer_count, out_width, in_width)
    half_turn = jnp.einsum('qlab,lbd->qlad', grid_form, in_basis, precision=precise)
    rotated = jnp.einsum('qlad,lac->qlcd', half_turn, out_basis, precision=precise)
    scaled = rotated / eigenvalues.reshape(layer_count, out_width, in_width)
    back_half = jnp.einsum('qlcd,led->qlce', scaled, in_basis, precision=precise)
    result = jnp.einsum('qlce,lac->qlae', back_half, out_basis, precision=precise)
    return result.reshape(row_total, layer_count, proj_width).astype(jnp.bfloat16)

def reference(train_grads, query_grads, out_basis, in_basis, eigenvalues, block_order):
    layer_count = train_grads.shape[1]
    proj_width = train_grads.shape[2]
    factor = 1.0 / math.sqrt(layer_count * proj_width)
    outputs = []
    for step_index in range(STEPS):
        raw_rows = lax.dynamic_index_in_dim(query_grads, block_order[step_index], 0, keepdims=False)
        ready = precondition(raw_rows, out_basis, in_basis, eigenvalues)

        def add_layer(total, layer_index):
            train_slice = lax.dynamic_index_in_dim(train_grads, layer_index, 1, keepdims=False)
            query_slice = lax.dynamic_index_in_dim(ready, layer_index, 1, keepdims=False)
            product = lax.dot_general(query_slice, train_slice, (((1,), (1,)), ((), ())), preferred_element_type=jnp.float32)
            return (total + product, None)
        start_total = jnp.zeros((ready.shape[0], train_grads.shape[0]), jnp.float32)
        totals, unused = lax.scan(add_layer, start_total, jnp.arange(layer_count, dtype=jnp.int32))
        outputs.append(totals * factor)
    return jnp.stack(outputs)
```

```python
import math

import jax
import jax.numpy as jnp
from jax import lax
from jax.experimental import pallas as pl
from jax.experimental.pallas import tpu as pltpu
from jax.sharding import PartitionSpec as P

STEPS = 3
MESH = pl.DeviceIdType.MESH
F32 = jnp.float32
BF16 = jnp.bfloat16
LATE = 5
CATCH = 6


def mm(a, b):
    return lax.dot_general(a, b, (((1,), (0,)), ((), ())), preferred_element_type=F32)


def split(x, parts):
    out = []
    for _ in range(parts):
        top = x.astype(BF16)
        out.append(top)
        x = x - top.astype(F32)
    return out


def mm3(x, y):
    return mm(x[0], y[0]) + (mm(x[0], y[1]) + mm(x[1], y[0]))


def twice(m):
    zero = jnp.zeros_like(m)
    return jnp.concatenate(
        [jnp.concatenate([m, zero], axis=1), jnp.concatenate([zero, m], axis=1)], axis=0
    )


def spread(m_parts):
    rows = lax.broadcasted_iota(jnp.int32, (512, 64), 0)
    cols = lax.broadcasted_iota(jnp.int32, (512, 64), 1)
    pick_row = ((rows // 256) + 2 * ((rows % 256) // 8) == cols).astype(F32).astype(BF16)
    k_rows = lax.broadcasted_iota(jnp.int32, (64, 512), 0)
    k_cols = lax.broadcasted_iota(jnp.int32, (64, 512), 1)
    pick_col = ((k_cols // 256) + 2 * ((k_cols % 256) // 8) == k_rows).astype(F32).astype(BF16)
    row_q = lax.broadcasted_iota(jnp.int32, (512, 512), 0) % 8
    col_q = lax.broadcasted_iota(jnp.int32, (512, 512), 1) % 8
    same = row_q == col_q
    out = []
    for part in m_parts:
        tall = mm(pick_row, part).astype(BF16)
        full = mm(tall, pick_col)
        out.append(jnp.where(same, full, 0.0).astype(BF16))
    return out


def left_apply(kron_parts, blocks):
    lane = lax.broadcasted_iota(jnp.int32, (256, 128), 1)
    low = lane < 64

    def turn(v):
        return pltpu.roll(v, 64, 1)

    b0, b1, b2 = blocks
    even = jnp.concatenate([jnp.where(low, b0, turn(b1)), b2], axis=1)
    odd = jnp.concatenate([jnp.where(low, turn(b0), b1), turn(b2)], axis=1)
    right = jnp.concatenate([even, odd], axis=0)
    out = mm3(kron_parts, split(right, 2))
    top, bot = out[:256], out[256:]
    r0 = jnp.where(low, top[:, :128], turn(bot[:, :128]))
    r1 = jnp.where(low, turn(top[:, :128]), bot[:, :128])
    r2 = jnp.where(low, top[:, 128:], turn(bot[:, 128:]))
    return r0, r1, r2


def stack_groups(x, count):
    return jnp.concatenate([x[:, g * 128 : (g + 1) * 128] for g in range(count)], axis=0)


def unstack_groups(x, first, count):
    return jnp.concatenate([x[(first + g) * 8 : (first + g + 1) * 8] for g in range(count)], axis=1)


def kernel(
    order_ref, train_ref, query_ref, a_ref, b_ref, lam_ref, out_ref,
    tbuf, qbuf, pf, xqs, xqr, own, ysend, ybuf, xsend, xbuf,
    train_sem, xq_ssem, xq_rsem, zs_ssem, c_ssem, z_rsem, c_rsem, y_ssem, y_rsem, x_ssem, x_rsem,
):
    dp = lax.axis_index("dp")
    layer = lax.axis_index("layer")
    z, h, c = dp // 4, (dp // 2) % 2, dp % 2
    lx, y = layer // 4, layer % 4
    x = 2 * h + lx

    def at(zz, hh, cc, ll, yy):
        return (4 * zz + 2 * hh + cc, 4 * ll + yy)

    def at_x(xx):
        return at(z, xx // 2, c, xx % 2, y)

    right, left = at((z + 1) % 16, h, c, lx, y), at((z + 15) % 16, h, c, lx, y)
    other_core = at(z, h, 1 - c, lx, y)
    partner = at(z, 1 - h, c, lx, y)
    y_peers = [at(z, h, c, lx, (y + k) % 4) for k in (1, 2, 3)]
    x_peers = [at_x((x + k) % 4) for k in (1, 2, 3)]

    barrier = pltpu.get_barrier_semaphore()
    everyone = [right, left, other_core] + y_peers + x_peers
    for device in everyone:
        pl.semaphore_signal(barrier, inc=1, device_id=device, device_id_type=MESH)

    def remote(src, dst, ssem, rsem, device):
        return pltpu.make_async_remote_copy(
            src_ref=src, dst_ref=dst, send_sem=ssem, recv_sem=rsem, device_id=device, device_id_type=MESH
        )

    half = 2048
    local_train = pltpu.make_async_copy(
        train_ref.at[:, pl.ds(pl.multiple_of(h * half, half), half)], tbuf.at[h], train_sem.at[0]
    )
    local_train.start()

    b_mat = b_ref[0]
    a_mat = a_ref[0]
    forth = split(twice(b_mat), 3)
    back = split(twice(b_mat.T), 2)
    a_parts = split(a_mat, 2)
    at_parts = split(a_mat.T, 2)
    kron_in = spread(at_parts)
    kron_out = spread(a_parts)
    lam = lam_ref[...]
    lam_rows = jnp.concatenate(
        [jnp.broadcast_to(lam[:, g * 128 : (g + 1) * 128], (8, 128)) for g in range(32)], axis=0
    )
    first = []
    for s in range(STEPS):
        raw = stack_groups(query_ref[order_ref[s]].astype(F32), 32).astype(BF16)
        first.append(mm(raw, forth[0]) + (mm(raw, forth[1]) + mm(raw, forth[2])))
    rotated = left_apply(kron_in, first)
    scaled = [mm3(split(r / lam_rows, 2), back) for r in rotated]
    ready = left_apply(kron_out, scaled)
    for s in range(STEPS):
        pf[s, 0] = ready[s][:128]
        pf[s, 1] = ready[s][128:]

    pl.semaphore_wait(barrier, len(everyone))

    def xq(s):
        return remote(xqs.at[s], xqr.at[s], xq_ssem.at[s], xq_rsem.at[s], partner)

    for s in range(STEPS):
        away = pf[s, 1 - h]
        xqs[s] = jnp.concatenate(
            [unstack_groups(away, 0, 8), unstack_groups(away, 8, 8)], axis=0
        ).astype(BF16)
        xq(s).start()
    send_train = remote(
        train_ref.at[:, pl.ds(pl.multiple_of((1 - h) * half, half), half)],
        tbuf.at[h], train_sem.at[1], train_sem.at[2], partner,
    )
    send_train.start()

    def ring(zs, s, way, t):
        slot = qbuf.at[zs, c, s]
        return remote(slot, slot, zs_ssem.at[way, t, s], z_rsem.at[zs, s], right if way == 0 else left)

    def hand(zs, s):
        slot = qbuf.at[zs, c, s]
        return remote(slot, slot, c_ssem.at[zs, s], c_rsem.at[zs, s], other_core)

    def handed(zs, s):
        slot = qbuf.at[zs, 1 - c, s]
        return remote(slot, slot, c_ssem.at[zs, s], c_rsem.at[zs, s], other_core)

    for s in range(STEPS):
        here = unstack_groups(pf[s, h], 0, 16)
        xq(s).wait_recv()
        got = xqr[s].astype(F32)
        there = jnp.concatenate([got[:8], got[8:]], axis=1)
        slot = jnp.where(
            h == 0, jnp.concatenate([here, there], axis=0), jnp.concatenate([there, here], axis=0)
        )
        qbuf[z, c, s] = slot.astype(BF16)
        ring(z, s, 0, 0).start()
        ring(z, s, 1, 0).start()
        hand(z, s).start()

    def chunk(m):
        return (z + 16 + (1 - 2 * (m % 2)) * ((m + 1) // 2)) % 16

    def y_copy(zs, e):
        k = zs % 2 + 2 * (zs // 8)
        to = (zs // 2) % 4
        return remote(
            ysend.at[zs, e], ybuf.at[k, y, e], y_ssem.at[zs, e], y_rsem.at[k, y, e], at(z, h, c, lx, to)
        )

    def score(m, e, fresh):
        zs = chunk(m)
        if fresh:
            for s in range(STEPS):
                handed(zs, s).wait_recv()
        lhs = qbuf[zs].reshape(96, half)
        part = lax.dot_general(lhs, tbuf[e], (((1,), (1,)), ((), ())), preferred_element_type=F32)
        k = zs % 2 + 2 * (zs // 8)

        @pl.when((zs // 2) % 4 == y)
        def _():
            own[k, e] = part

        @pl.when((zs // 2) % 4 != y)
        def _():
            ysend[zs, e] = part.astype(BF16)
            y_copy(zs, e).start()

    def x_copy(zs, e):
        k = zs % 2 + 2 * (zs // 8)
        return remote(
            xsend.at[k, e], xbuf.at[zs % 2, x], x_ssem.at[k, e], x_rsem.at[zs % 2, x],
            at(z, e, c, zs // 8, y),
        )

    def join(m, e):
        zs = chunk(m)
        k = zs % 2 + 2 * (zs // 8)

        @pl.when((zs // 2) % 4 == y)
        def _():
            total = own[k, e]
            for step in (1, 2, 3):
                src = (y + step) % 4
                slot = ybuf.at[k, src, e]
                remote(slot, slot, y_ssem.at[zs, e], y_rsem.at[k, src, e], right).wait_recv()
                total = total + ybuf[k, src, e].astype(F32)
            mine = 2 * e + zs // 8 == x

            @pl.when(mine)
            def _():
                xbuf[zs % 2, x] = total

            @pl.when(jnp.logical_not(mine))
            def _():
                xsend[k, e] = total
                x_copy(zs, e).start()

    def over(lo, hi, f):
        if hi > lo:

            @pl.loop(lo, hi)
            def _(m):
                f(m)

    waiting = []
    caught = 0
    for t in range(1, 9):
        for s in range(STEPS):
            if t < 8:
                for way in (0, 1):
                    zs = (z + 16 - t) % 16 if way == 0 else (z + t) % 16
                    ring(zs, s, way, t).wait_recv()
                    if t < 7 or (way == 0 and s == 0) or (way == 1 and s == 2):
                        ring(zs, s, way, t).start()
                    elif s == 1:

                        @pl.when(c == way)
                        def _():
                            ring(zs, s, way, t).start()

                    hand(zs, s).start()
            else:
                zs = (z + 8) % 16
                ring(zs, s, 0, 0).wait_recv()
                hand(zs, s).start()
        if t == 1:
            local_train.wait()
        lo, hi = max(2 * t - 3, 0), 2 * t - 1
        over(lo, hi, lambda m: score(m, h, True))
        done = [(lo, hi, True)]
        if t >= LATE:
            if t == LATE:
                local = tbuf.at[1 - h]
                remote(local, local, train_sem.at[1], train_sem.at[2], partner).wait_recv()
            top = min(caught + CATCH, hi)
            over(caught, top, lambda m: score(m, 1 - h, False))
            done.append((caught, top, False))
            caught = top
        for lo, hi, mine in waiting:
            over(lo, hi, lambda m: join(m, h if mine else 1 - h))
        waiting = done
    score(15, h, True)
    score(15, 1 - h, False)
    for lo, hi, mine in waiting + [(15, 16, True), (15, 16, False)]:
        over(lo, hi, lambda m: join(m, h if mine else 1 - h))

    factor = 1.0 / math.sqrt(8 * 4096)
    for j in (0, 1):
        total = xbuf[j, x]
        for step in (1, 2, 3):
            src = (x + step) % 4
            slot = xbuf.at[j, src]
            remote(slot, slot, x_ssem.at[0, 0], x_rsem.at[j, src], right).wait_recv()
            total = total + xbuf[j, src]
        total = total * factor
        for cc in range(2):
            for s in range(STEPS):
                for hh in range(2):
                    row = cc * 48 + s * 16 + hh * 8
                    to = 32 * j + 16 * hh + 8 * cc
                    out_ref[s, to : to + 8, :] = total[row : row + 8]

    send_train.wait_send()
    for s in range(STEPS):
        xq(s).wait_send()
        for t in range(8):
            for way in (0, 1):
                zs = (z + 16 - t) % 16 if way == 0 else (z + t) % 16
                if t < 7 or (way == 0 and s == 0) or (way == 1 and s == 2):
                    ring(zs, s, way, t).wait_send()
                elif s == 1:

                    @pl.when(c == way)
                    def _():
                        ring(zs, s, way, t).wait_send()

    @pl.loop(0, 16)
    def _(zs):
        for s in range(STEPS):
            hand(zs, s).wait_send()
        for e in (0, 1):

            @pl.when((zs // 2) % 4 != y)
            def _():
                y_copy(zs, e).wait_send()

            @pl.when(((zs // 2) % 4 == y) & (2 * e + zs // 8 != x))
            def _():
                x_copy(zs, e).wait_send()


def body(train_grads, query_grads, out_basis, in_basis, eigenvalues, block_order):
    train = train_grads.reshape(256, 4096)
    query = query_grads.reshape(4, 8, 4096)
    vmem = pl.BlockSpec(memory_space=pltpu.VMEM)
    dma = pltpu.SemaphoreType.DMA
    return pl.pallas_call(
        kernel,
        out_shape=jax.ShapeDtypeStruct((STEPS, 64, 256), F32),
        in_specs=[
            pl.BlockSpec(memory_space=pltpu.SMEM),
            pl.BlockSpec(memory_space=pl.ANY),
            vmem, vmem, vmem, vmem,
        ],
        out_specs=vmem,
        scratch_shapes=[
            pltpu.VMEM((2, 256, 2048), BF16),
            pltpu.VMEM((16, 2, 3, 16, 2048), BF16),
            pltpu.VMEM((3, 2, 128, 128), F32),
            pltpu.VMEM((3, 16, 1024), BF16),
            pltpu.VMEM((3, 16, 1024), BF16),
            pltpu.VMEM((4, 2, 96, 256), F32),
            pltpu.VMEM((16, 2, 96, 256), BF16),
            pltpu.VMEM((4, 4, 2, 96, 256), BF16),
            pltpu.VMEM((4, 2, 96, 256), F32),
            pltpu.VMEM((2, 4, 96, 256), F32),
            dma((3,)), dma((3,)), dma((3,)),
            dma((2, 8, 3)), dma((16, 3)), dma((16, 3)), dma((16, 3)),
            dma((16, 2)), dma((4, 4, 2)), dma((4, 2)), dma((2, 4)),
        ],
        compiler_params=pltpu.CompilerParams(
            collective_id=0, has_side_effects=True, vmem_limit_bytes=48 << 20
        ),
    )(block_order, train, query, out_basis, in_basis, eigenvalues)


def solution(mesh):
    placed = (
        P("dp", "layer", None),
        P(None, "dp", "layer", None),
        P("layer", None, None),
        P("layer", None, None),
        P("layer", None),
        P(),
    )
    return jax.shard_map(
        body, mesh=mesh, in_specs=placed, out_specs=P(None, "layer", "dp"), check_vma=False
    )
```

```python
import math

import jax
import jax.numpy as jnp
from jax import lax
from jax.experimental import pallas as pl
from jax.experimental.pallas import tpu as pltpu
from jax.sharding import PartitionSpec as P

STEPS = 3
MESH = pl.DeviceIdType.MESH
F32 = jnp.float32
BF16 = jnp.bfloat16
LAG_Y = 2
LAG_X = 2
LATE = 5
CATCH = 6


def mm(a, b):
    return lax.dot_general(a, b, (((1,), (0,)), ((), ())), preferred_element_type=F32)


def split(x, parts):
    out = []
    for _ in range(parts):
        top = x.astype(BF16)
        out.append(top)
        x = x - top.astype(F32)
    return out


def mm3(x, y):
    return mm(x[0], y[0]) + (mm(x[0], y[1]) + mm(x[1], y[0]))


def twice(m):
    zero = jnp.zeros_like(m)
    return jnp.concatenate(
        [jnp.concatenate([m, zero], axis=1), jnp.concatenate([zero, m], axis=1)], axis=0
    )


def spread(m_parts):
    rows = lax.broadcasted_iota(jnp.int32, (512, 64), 0)
    cols = lax.broadcasted_iota(jnp.int32, (512, 64), 1)
    pick_row = ((rows // 256) + 2 * ((rows % 256) // 8) == cols).astype(F32).astype(BF16)
    k_rows = lax.broadcasted_iota(jnp.int32, (64, 512), 0)
    k_cols = lax.broadcasted_iota(jnp.int32, (64, 512), 1)
    pick_col = ((k_cols // 256) + 2 * ((k_cols % 256) // 8) == k_rows).astype(F32).astype(BF16)
    row_q = lax.broadcasted_iota(jnp.int32, (512, 512), 0) % 8
    col_q = lax.broadcasted_iota(jnp.int32, (512, 512), 1) % 8
    same = row_q == col_q
    out = []
    for part in m_parts:
        tall = mm(pick_row, part).astype(BF16)
        full = mm(tall, pick_col)
        out.append(jnp.where(same, full, 0.0).astype(BF16))
    return out


def left_apply(kron_parts, blocks):
    lane = lax.broadcasted_iota(jnp.int32, (256, 128), 1)
    low = lane < 64

    def turn(v):
        return pltpu.roll(v, 64, 1)

    b0, b1, b2 = blocks
    even = jnp.concatenate([jnp.where(low, b0, turn(b1)), b2], axis=1)
    odd = jnp.concatenate([jnp.where(low, turn(b0), b1), turn(b2)], axis=1)
    right = jnp.concatenate([even, odd], axis=0)
    out = mm3(kron_parts, split(right, 2))
    top, bot = out[:256], out[256:]
    r0 = jnp.where(low, top[:, :128], turn(bot[:, :128]))
    r1 = jnp.where(low, turn(top[:, :128]), bot[:, :128])
    r2 = jnp.where(low, top[:, 128:], turn(bot[:, 128:]))
    return r0, r1, r2


def stack_groups(x, count):
    return jnp.concatenate([x[:, g * 128 : (g + 1) * 128] for g in range(count)], axis=0)


def unstack_groups(x, first, count):
    return jnp.concatenate([x[(first + g) * 8 : (first + g + 1) * 8] for g in range(count)], axis=1)


def kernel(
    order_hbm, train_ref, query_hbm, a_hbm, b_hbm, lam_hbm, out_ref,
    order_ref, query_ref, a_ref, b_ref, lam_ref, in_sem, tbuf, qbuf, pf, xqs, xqr, own, ysend, ybuf, xsend, xbuf, fsend, fbuf,
    train_sem, xq_ssem, xq_rsem, zs_ssem, c_ssem, z_rsem, c_rsem, y_ssem, y_rsem, x_ssem, x_rsem, f_ssem, f_rsem,
):
    dp = lax.axis_index("dp")
    layer = lax.axis_index("layer")
    z, h, c = dp // 4, (dp // 2) % 2, dp % 2
    lx, y = layer // 4, layer % 4
    x = 2 * h + lx

    def at(zz, hh, cc, ll, yy):
        return (4 * zz + 2 * hh + cc, 4 * ll + yy)

    copies = [
        pltpu.make_async_copy(src, dst, in_sem.at[i])
        for i, (src, dst) in enumerate(
            [
                (a_hbm, a_ref), (b_hbm, b_ref), (query_hbm, query_ref),
                (order_hbm, order_ref), (lam_hbm, lam_ref),
            ]
        )
    ]
    for copy in copies:
        copy.start()

    def at_x(xx):
        return at(z, xx // 2, c, xx % 2, y)

    right, left = at((z + 1) % 16, h, c, lx, y), at((z + 15) % 16, h, c, lx, y)
    other_core = at(z, h, 1 - c, lx, y)
    partner = at(z, 1 - h, c, lx, y)

    barrier = pltpu.get_barrier_semaphore()
    everyone = [right, left, other_core]
    for step in (1, 2, 3):
        aside = (y + step) % 4
        everyone += [at(z, h, c, lx, aside), at(z, h, c, 1 - lx, aside), at_x((x + step) % 4)]
    for device in everyone:
        pl.semaphore_signal(barrier, inc=1, device_id=device, device_id_type=MESH)

    def remote(src, dst, ssem, rsem, device):
        return pltpu.make_async_remote_copy(
            src_ref=src, dst_ref=dst, send_sem=ssem, recv_sem=rsem, device_id=device, device_id_type=MESH
        )

    half = 2048
    local_train = pltpu.make_async_copy(
        train_ref.at[:, pl.ds(pl.multiple_of(h * half, half), half)], tbuf.at[h], train_sem.at[0]
    )
    local_train.start()

    copies[0].wait()
    copies[1].wait()
    b_mat = b_ref[0]
    a_mat = a_ref[0]
    forth = split(twice(b_mat), 3)
    back = split(twice(b_mat.T), 2)
    a_parts = split(a_mat, 2)
    at_parts = split(a_mat.T, 2)
    kron_in = spread(at_parts)
    kron_out = spread(a_parts)
    for copy in copies[2:]:
        copy.wait()
    lam = lam_ref[...]
    lam_rows = jnp.concatenate(
        [jnp.broadcast_to(lam[:, g * 128 : (g + 1) * 128], (8, 128)) for g in range(32)], axis=0
    )
    first = []
    for s in range(STEPS):
        raw = stack_groups(query_ref[order_ref[s]].astype(F32), 32).astype(BF16)
        first.append(mm(raw, forth[0]) + (mm(raw, forth[1]) + mm(raw, forth[2])))
    rotated = left_apply(kron_in, first)
    scaled = [mm3(split(r / lam_rows, 2), back) for r in rotated]
    ready = left_apply(kron_out, scaled)
    for s in range(STEPS):
        pf[s, 0] = ready[s][:128]
        pf[s, 1] = ready[s][128:]

    pl.semaphore_wait(barrier, len(everyone))

    def xq(s):
        return remote(xqs.at[s], xqr.at[s], xq_ssem.at[s], xq_rsem.at[s], partner)

    for s in range(STEPS):
        away = pf[s, 1 - h]
        xqs[s] = jnp.concatenate(
            [unstack_groups(away, 0, 8), unstack_groups(away, 8, 8)], axis=0
        ).astype(BF16)
        xq(s).start()
    send_train = remote(
        train_ref.at[:, pl.ds(pl.multiple_of((1 - h) * half, half), half)],
        tbuf.at[h], train_sem.at[1], train_sem.at[2], partner,
    )
    send_train.start()

    def ring(zs, s, way, t):
        slot = qbuf.at[zs, c, s]
        return remote(slot, slot, zs_ssem.at[way, t, s], z_rsem.at[zs, s], right if way == 0 else left)

    def hand(zs, s):
        slot = qbuf.at[zs, c, s]
        return remote(slot, slot, c_ssem.at[zs, s], c_rsem.at[zs, s], other_core)

    def handed(zs, s):
        slot = qbuf.at[zs, 1 - c, s]
        return remote(slot, slot, c_ssem.at[zs, s], c_rsem.at[zs, s], other_core)

    for s in range(STEPS):
        here = unstack_groups(pf[s, h], 0, 16)
        xq(s).wait_recv()
        got = xqr[s].astype(F32)
        there = jnp.concatenate([got[:8], got[8:]], axis=1)
        slot = jnp.where(
            h == 0, jnp.concatenate([here, there], axis=0), jnp.concatenate([there, here], axis=0)
        )
        qbuf[z, c, s] = slot.astype(BF16)
        ring(z, s, 0, 0).start()
        ring(z, s, 1, 0).start()
        hand(z, s).start()

    def chunk(m):
        return (z + 16 + (1 - 2 * (m % 2)) * ((m + 1) // 2)) % 16

    def owner(m, cs, e):
        return 2 * (e if isinstance(m, int) and m in (0, 15) else m % 2) + cs

    def y_copy(m, cs, e):
        zs, t, to = chunk(m), (m + 1) // 2, owner(m, cs, e)
        return remote(
            ysend.at[zs, e, cs], ybuf.at[t, e, y], y_ssem.at[zs, e, cs], y_rsem.at[t, e, y],
            at(z, h, c, lx, to),
        )

    def score(m, e, fresh):
        zs = chunk(m)
        if fresh:
            for s in range(STEPS):
                handed(zs, s).wait_recv()
        lhs = qbuf[zs].reshape(96, half)
        part = lax.dot_general(lhs, tbuf[e], (((1,), (1,)), ((), ())), preferred_element_type=F32)
        for cs in (0, 1):
            rows = part[48 * cs : 48 * cs + 48]

            @pl.when(owner(m, cs, e) == y)
            def _():
                own[(m + 1) // 2, e] = rows

            @pl.when(owner(m, cs, e) != y)
            def _():
                ysend[zs, e, cs] = rows.astype(BF16)
                y_copy(m, cs, e).start()

    def x_copy(m, e, col):
        t = (m + 1) // 2
        return remote(
            xsend.at[t, e, col], xbuf.at[t, x], x_ssem.at[t, e, col], x_rsem.at[t, x], at_x(2 * e + col)
        )

    def f_copy(m):
        zs, t = chunk(m), (m + 1) // 2
        return remote(
            fsend.at[t], fbuf.at[zs % 2, y % 2, lx], f_ssem.at[t], f_rsem.at[zs % 2, y % 2, lx],
            at(z, h, c, zs // 8, (zs // 2) % 4),
        )

    def join(m, e):
        zs, t = chunk(m), (m + 1) // 2

        @pl.when(owner(m, y % 2, e) == y)
        def _():
            total = own[t, e]
            for step in (1, 2, 3):
                src = (y + step) % 4
                slot = ybuf.at[t, e, src]
                remote(slot, slot, y_ssem.at[zs, e, 0], y_rsem.at[t, e, src], right).wait_recv()
                total = total + ybuf[t, e, src].astype(F32)
            for col in (0, 1):
                part = total[:, 128 * col : 128 * col + 128].astype(xsend.dtype)

                @pl.when(2 * e + col == x)
                def _():
                    xbuf[t, x] = part

                @pl.when(2 * e + col != x)
                def _():
                    xsend[t, e, col] = part
                    x_copy(m, e, col).start()

    def kept(m):
        zs = chunk(m)
        return ((zs // 2) % 4 == y) & (zs // 8 == lx)

    def finish(m):
        zs, t = chunk(m), (m + 1) // 2

        @pl.when(owner(m, y % 2, h) == y)
        def _():
            total = xbuf[t, x].astype(F32)
            for step in (1, 2, 3):
                src = (x + step) % 4
                slot = xbuf.at[t, src]
                remote(slot, slot, x_ssem.at[t, 0, 0], x_rsem.at[t, src], right).wait_recv()
                total = total + xbuf[t, src].astype(F32)

            @pl.when(kept(m))
            def _():
                fbuf[zs % 2, y % 2, lx] = total

            @pl.when(jnp.logical_not(kept(m)))
            def _():
                fsend[t] = total
                f_copy(m).start()

    def over(lo, hi, f):
        for edge in (0, 15):
            if lo <= edge < hi:
                f(edge)
        lo, hi = max(lo, 1), min(hi, 15)
        if hi > lo:

            @pl.loop(lo, hi)
            def _(m):
                f(m)

    def pass_on(t, s):
        for way in (0, 1):
            zs = (z + 16 - t) % 16 if way == 0 else (z + t) % 16
            ring(zs, s, way, t).wait_recv()
            if t < 7 or (way == 0 and s == 0) or (way == 1 and s == 2):
                ring(zs, s, way, t).start()
            elif s == 1:

                @pl.when(c == way)
                def _():
                    ring(zs, s, way, t).start()

            hand(zs, s).start()

    def mine(lo, hi):
        over(lo, hi, lambda m: score(m, h, True))

    def theirs(lo, hi):
        over(lo, hi, lambda m: score(m, 1 - h, False))

    def joins(items):
        for lo, hi, e in items:
            over(lo, hi, lambda m: join(m, e))

    def finishes(items):
        for lo, hi, e in items:
            if e is not h:
                over(lo, hi, finish)

    scored, joined = [], []
    caught = 0
    not_h = 1 - h

    def settle(t):
        while scored and scored[0][0] + LAG_Y <= t:
            _, lo, hi, e = scored.pop(0)
            joins([(lo, hi, e)])
            joined.append((t, lo, hi, e))
        while joined and joined[0][0] + LAG_X <= t:
            finishes([joined.pop(0)[1:]])

    for t in range(1, 8):
        pass_on(t, 0)
        if t == 1:
            local_train.wait()
        settle(t)
        pass_on(t, 1)
        lo, hi = max(2 * t - 3, 0), 2 * t - 1
        mine(lo, hi)
        scored.append((t, lo, hi, h))
        pass_on(t, 2)
        if t >= LATE:
            if t == LATE:
                local = tbuf.at[1 - h]
                remote(local, local, train_sem.at[1], train_sem.at[2], partner).wait_recv()
            top = min(caught + CATCH, hi)
            theirs(caught, top)
            scored.append((t, caught, top, not_h))
            caught = top
    mine(13, 15)
    theirs(caught, 15)
    for s in range(STEPS):
        ring((z + 8) % 16, s, 0, 0).wait_recv()
        hand((z + 8) % 16, s).start()
    settle(7 + LAG_Y - 1)
    mine(15, 16)
    theirs(15, 16)
    settle(7 + LAG_Y)
    joins([(13, 15, h), (caught, 15, not_h)])
    finishes([item[1:] for item in joined])
    joins([(15, 16, h), (15, 16, not_h)])
    finishes([(caught, 15, not_h)])
    finishes([(15, 16, not_h)])

    factor = 1.0 / math.sqrt(8 * 4096)
    for j in (0, 1):
        ahead = (2 * layer + j - z + 16) % 16
        edge = (ahead == 0) | (ahead == 8)
        group = jnp.where(edge, h, jnp.where(ahead > 8, 1, 0))
        for cs in (0, 1):
            for col in (0, 1):
                slot = fbuf.at[j, cs, col]

                @pl.when((2 * group + cs != y) | (col != lx))
                def _():
                    remote(slot, slot, f_ssem.at[0], f_rsem.at[j, cs, col], right).wait_recv()

                total = fbuf[j, cs, col] * factor
                for s in range(STEPS):
                    for hh in range(2):
                        to = 32 * j + 16 * hh + 8 * cs
                        row = 16 * s + 8 * hh
                        out_ref[s, to : to + 8, 128 * col : 128 * col + 128] = total[row : row + 8]

    send_train.wait_send()
    for s in range(STEPS):
        xq(s).wait_send()
        for t in range(8):
            for way in (0, 1):
                zs = (z + 16 - t) % 16 if way == 0 else (z + t) % 16
                if t < 7 or (way == 0 and s == 0) or (way == 1 and s == 2):
                    ring(zs, s, way, t).wait_send()
                elif s == 1:

                    @pl.when(c == way)
                    def _():
                        ring(zs, s, way, t).wait_send()

    @pl.loop(0, 16)
    def _(zs):
        for s in range(STEPS):
            hand(zs, s).wait_send()

    def sent(m):
        for e in (0, 1):
            for cs in (0, 1):

                @pl.when(owner(m, cs, e) != y)
                def _():
                    y_copy(m, cs, e).wait_send()

            for col in (0, 1):

                @pl.when((owner(m, y % 2, e) == y) & (2 * e + col != x))
                def _():
                    x_copy(m, e, col).wait_send()

        @pl.when((owner(m, y % 2, h) == y) & jnp.logical_not(kept(m)))
        def _():
            f_copy(m).wait_send()

    over(0, 16, sent)


def body(train_grads, query_grads, out_basis, in_basis, eigenvalues, block_order):
    train = train_grads.reshape(256, 4096)
    query = query_grads.reshape(4, 8, 4096)
    dma = pltpu.SemaphoreType.DMA
    return pl.pallas_call(
        kernel,
        out_shape=jax.ShapeDtypeStruct((STEPS, 64, 256), F32),
        in_specs=[pl.BlockSpec(memory_space=pltpu.HBM)] * 6,
        out_specs=pl.BlockSpec(memory_space=pltpu.VMEM),
        scratch_shapes=[
            pltpu.SMEM((4,), jnp.int32),
            pltpu.VMEM((4, 8, 4096), BF16),
            pltpu.VMEM((1, 64, 64), F32),
            pltpu.VMEM((1, 64, 64), F32),
            pltpu.VMEM((1, 4096), F32),
            dma((5,)),
            pltpu.VMEM((2, 256, 2048), BF16),
            pltpu.VMEM((16, 2, 3, 16, 2048), BF16),
            pltpu.VMEM((3, 2, 128, 128), F32),
            pltpu.VMEM((3, 16, 1024), BF16),
            pltpu.VMEM((3, 16, 1024), BF16),
            pltpu.VMEM((9, 2, 48, 256), F32),
            pltpu.VMEM((16, 2, 2, 48, 256), BF16),
            pltpu.VMEM((9, 2, 4, 48, 256), BF16),
            pltpu.VMEM((9, 2, 2, 48, 128), F32),
            pltpu.VMEM((9, 4, 48, 128), F32),
            pltpu.VMEM((9, 48, 128), F32),
            pltpu.VMEM((2, 2, 2, 48, 128), F32),
            dma((3,)), dma((3,)), dma((3,)),
            dma((2, 8, 3)), dma((16, 3)), dma((16, 3)), dma((16, 3)),
            dma((16, 2, 2)), dma((9, 2, 4)), dma((9, 2, 2)), dma((9, 4)), dma((9,)), dma((2, 2, 2)),
        ],
        compiler_params=pltpu.CompilerParams(
            collective_id=0, has_side_effects=True, vmem_limit_bytes=63 << 20
        ),
    )(block_order, train, query, out_basis, in_basis, eigenvalues)


def solution(mesh):
    placed = (
        P("dp", "layer", None),
        P(None, "dp", "layer", None),
        P("layer", None, None),
        P("layer", None, None),
        P("layer", None),
        P(),
    )
    return jax.shard_map(
        body, mesh=mesh, in_specs=placed, out_specs=P(None, "layer", "dp"), check_vma=False
    )
```

```python
import math

import jax
import jax.numpy as jnp
from jax import lax
from jax.experimental import pallas as pl
from jax.experimental.pallas import tpu as pltpu
from jax.sharding import PartitionSpec as P

STEPS = 3
MESH = pl.DeviceIdType.MESH
F32 = jnp.float32
BF16 = jnp.bfloat16
EDGES = (0, 32, 256)
LAG_Y = 2
LAG_X = 2
LATE = 5
CATCH = 3


def mm(a, b):
    return lax.dot_general(a, b, (((1,), (0,)), ((), ())), preferred_element_type=F32)


def split(x, parts):
    out = []
    for _ in range(parts):
        top = x.astype(BF16)
        out.append(top)
        x = x - top.astype(F32)
    return out


def mm3(x, y):
    return mm(x[0], y[0]) + (mm(x[0], y[1]) + mm(x[1], y[0]))


def twice(m):
    zero = jnp.zeros_like(m)
    return jnp.concatenate(
        [jnp.concatenate([m, zero], axis=1), jnp.concatenate([zero, m], axis=1)], axis=0
    )


def patterns():
    rows = lax.broadcasted_iota(jnp.int32, (512, 64), 0)
    cols = lax.broadcasted_iota(jnp.int32, (512, 64), 1)
    pick_row = ((rows >> 8) + 2 * ((rows & 255) >> 3) == cols).astype(F32).astype(BF16)
    k_rows = lax.broadcasted_iota(jnp.int32, (64, 512), 0)
    k_cols = lax.broadcasted_iota(jnp.int32, (64, 512), 1)
    pick_col = ((k_cols >> 8) + 2 * ((k_cols & 255) >> 3) == k_rows).astype(F32).astype(BF16)
    row_q = lax.broadcasted_iota(jnp.int32, (512, 512), 0) & 7
    col_q = lax.broadcasted_iota(jnp.int32, (512, 512), 1) & 7
    return pick_row, pick_col, row_q == col_q


def spread(m_parts, pick_row, pick_col, same):
    out = []
    for part in m_parts:
        tall = mm(pick_row, part).astype(BF16)
        full = mm(tall, pick_col)
        out.append(jnp.where(same, full, 0.0).astype(BF16))
    return out


def left_apply(kron_parts, blocks):
    lane = lax.broadcasted_iota(jnp.int32, (256, 128), 1)
    low = lane < 64

    def turn(v):
        return pltpu.roll(v, 64, 1)

    b0, b1, b2 = blocks
    even = jnp.concatenate([jnp.where(low, b0, turn(b1)), b2], axis=1)
    odd = jnp.concatenate([jnp.where(low, turn(b0), b1), turn(b2)], axis=1)
    right = jnp.concatenate([even, odd], axis=0)
    out = mm3(kron_parts, split(right, 2))
    top, bot = out[:256], out[256:]
    r0 = jnp.where(low, top[:, :128], turn(bot[:, :128]))
    r1 = jnp.where(low, turn(top[:, :128]), bot[:, :128])
    r2 = jnp.where(low, top[:, 128:], turn(bot[:, 128:]))
    return r0, r1, r2


def stack_groups(x, count):
    return jnp.concatenate([x[:, g * 128 : (g + 1) * 128] for g in range(count)], axis=0)


def unstack_groups(x, first, count):
    return jnp.concatenate([x[(first + g) * 8 : (first + g + 1) * 8] for g in range(count)], axis=1)


def kernel(
    order_hbm, train_ref, query_hbm, a_hbm, b_hbm, lam_hbm, out_ref,
    order_ref, query_ref, a_ref, b_ref, lam_ref, in_sem, tbuf, qbuf, pf, xqs, own, ysend, ybuf, xsend, xbuf, fsend, fbuf,
    train_sem, train_ssem, train_rsem, xq_ssem, xq_rsem, zs_ssem, c_ssem, z_rsem, c_rsem, y_ssem, y_rsem, x_ssem, x_rsem, f_ssem, f_rsem,
):
    dp = lax.axis_index("dp")
    layer = lax.axis_index("layer")
    z, h, c = dp // 4, (dp // 2) % 2, dp % 2
    lx, y = layer // 4, layer % 4
    x = 2 * h + lx

    def at(zz, hh, cc, ll, yy):
        return (4 * zz + 2 * hh + cc, 4 * ll + yy)

    copies = [
        pltpu.make_async_copy(src, dst, in_sem.at[i])
        for i, (src, dst) in enumerate(
            [
                (a_hbm, a_ref), (b_hbm, b_ref), (query_hbm, query_ref),
                (order_hbm, order_ref), (lam_hbm, lam_ref),
            ]
        )
    ]
    for copy in copies:
        copy.start()

    def at_x(xx):
        return at(z, xx // 2, c, xx % 2, y)

    right, left = at((z + 1) % 16, h, c, lx, y), at((z + 15) % 16, h, c, lx, y)
    other_core = at(z, h, 1 - c, lx, y)
    partner = at(z, 1 - h, c, lx, y)

    barrier = pltpu.get_barrier_semaphore()
    everyone = [right, left, other_core]
    for step in (1, 2, 3):
        aside = (y + step) % 4
        everyone += [at(z, h, c, lx, aside), at(z, h, c, 1 - lx, aside), at_x((x + step) % 4)]
    for device in everyone:
        pl.semaphore_signal(barrier, inc=1, device_id=device, device_id_type=MESH)

    def remote(src, dst, ssem, rsem, device):
        return pltpu.make_async_remote_copy(
            src_ref=src, dst_ref=dst, send_sem=ssem, recv_sem=rsem, device_id=device, device_id_type=MESH
        )

    half = 2048
    local_train = pltpu.make_async_copy(
        train_ref.at[:, pl.ds(pl.multiple_of(h * half, half), half)], tbuf.at[h], train_sem
    )
    local_train.start()

    def train_copy(piece):
        rows = pl.ds(EDGES[piece], EDGES[piece + 1] - EDGES[piece])
        return remote(
            train_ref.at[rows, pl.ds(pl.multiple_of((1 - h) * half, half), half)],
            tbuf.at[h, rows], train_ssem.at[piece], train_rsem.at[piece], partner,
        )

    shapes = patterns()
    copies[0].wait()
    copies[1].wait()
    b_mat = b_ref[0]
    a_mat = a_ref[0]
    forth = split(twice(b_mat), 3)
    back = split(twice(b_mat.T), 2)
    a_parts = split(a_mat, 2)
    at_parts = split(a_mat.T, 2)
    kron_in = spread(at_parts, *shapes)
    kron_out = spread(a_parts, *shapes)
    for copy in copies[2:]:
        copy.wait()
    pl.semaphore_wait(barrier, len(everyone))
    train_copy(0).start()
    lam = lam_ref[...]
    lam_rows = jnp.concatenate(
        [jnp.broadcast_to(lam[:, g * 128 : (g + 1) * 128], (8, 128)) for g in range(32)], axis=0
    )
    first = []
    for s in range(STEPS):
        raw = stack_groups(query_ref[order_ref[s]].astype(F32), 32).astype(BF16)
        first.append(mm(raw, forth[0]) + (mm(raw, forth[1]) + mm(raw, forth[2])))
    rotated = left_apply(kron_in, first)
    scaled = [mm3(split(r / lam_rows, 2), back) for r in rotated]
    ready = left_apply(kron_out, scaled)
    for s in range(STEPS):
        pf[s, 0] = ready[s][:128]
        pf[s, 1] = ready[s][128:]


    def unit(zs, cc, u):
        hh = h if u < 2 else 1 - h
        return qbuf.at[zs, cc, hh, pl.ds(0, 32) if u % 2 == 0 else pl.ds(32, 16)]

    def ring(zs, u, way, t):
        slot = unit(zs, c, u)
        return remote(slot, slot, zs_ssem.at[way, t, u], z_rsem.at[zs, u], right if way == 0 else left)

    def hand(zs, u):
        slot = unit(zs, c, u)
        return remote(slot, slot, c_ssem.at[zs, u], c_rsem.at[zs, u], other_core)

    def handed(zs, u):
        slot = unit(zs, 1 - c, u)
        return remote(slot, slot, c_ssem.at[zs, u], c_rsem.at[zs, u], other_core)

    def xq(u):
        rows = pl.ds(0, 32) if u == 0 else pl.ds(32, 16)
        return remote(xqs.at[rows], qbuf.at[z, c, h, rows], xq_ssem.at[u], xq_rsem.at[u], partner)

    def xq_in(u):
        slot = unit(z, c, 2 + u)
        return remote(slot, slot, xq_ssem.at[u], xq_rsem.at[u], partner)

    def tall(part):
        return jnp.concatenate([unstack_groups(part, 0, 8), unstack_groups(part, 8, 8)], axis=0)

    def launch(u):
        ring(z, u, 0, 0).start()
        ring(z, u, 1, 0).start()
        hand(z, u).start()

    xqs[...] = jnp.concatenate([tall(pf[s, 1 - h]) for s in range(STEPS)], axis=0).astype(BF16)
    xq(0).start()
    xq(1).start()
    qbuf[z, c, h] = jnp.concatenate([tall(pf[s, h]) for s in range(STEPS)], axis=0).astype(BF16)
    launch(0)
    launch(1)
    train_copy(1).start()
    for u in (0, 1):
        xq_in(u).wait_recv()
        launch(2 + u)

    def lone(d):
        return isinstance(d, int) and d in (0, 8)

    def chunks(d):
        return [(z + d) % 16] if lone(d) else [(z + 16 - d) % 16, (z + d) % 16]

    def my_chunk(d):
        return (z + d) % 16 if lone(d) else (z + 16 + (1 - 2 * (y // 2)) * d) % 16

    def y_copy(d, e, to):
        return remote(
            ysend.at[d, e, to], ybuf.at[d, e, y], y_ssem.at[d, e, to], y_rsem.at[d, e, y],
            at(z, h, c, lx, to),
        )

    def wide(zs):
        rows = qbuf[zs].astype(F32).reshape(12, 16, 1024)
        low, high = rows[:, :8].reshape(96, 1024), rows[:, 8:].reshape(96, 1024)
        return jnp.concatenate([low, high], axis=1).astype(BF16)

    def score(d, e, fresh):
        held = chunks(d)
        if fresh:
            for zs in held:
                for u in range(4):
                    handed(zs, u).wait_recv()
        lhs = jnp.concatenate([wide(zs) for zs in held], axis=0)
        part = lax.dot_general(lhs, tbuf[e], (((1,), (1,)), ((), ())), preferred_element_type=F32)
        for piece in range(2 * len(held)):
            rows = part[48 * piece : 48 * piece + 48]
            to = 2 * e + piece if lone(d) else (2, 3, 0, 1)[piece]

            @pl.when(to == y)
            def _():
                own[d, e] = rows

            ysend[d, e, to] = rows.astype(BF16)
        for step in (1, 2, 3):
            to = (y + step) % 4
            if lone(d):

                @pl.when(to // 2 == e)
                def _():
                    y_copy(d, e, to).start()

            else:
                y_copy(d, e, to).start()

    def x_copy(d, e, col):
        return remote(
            xsend.at[d, e, col], xbuf.at[d, x], x_ssem.at[d, e, col], x_rsem.at[d, x], at_x(2 * e + col)
        )

    def f_copy(d):
        zs = my_chunk(d)
        return remote(
            fsend.at[d], fbuf.at[zs % 2, y % 2, lx], f_ssem.at[d], f_rsem.at[zs % 2, y % 2, lx],
            at(z, h, c, zs // 8, (zs // 2) % 4),
        )

    def guarded(d, e, f):
        if lone(d):
            pl.when(y // 2 == e)(f)
        else:
            f()

    def join(d, e):
        for step in (1, 2, 3):
            to = (y + step) % 4
            if lone(d):

                @pl.when(to // 2 == e)
                def _():
                    y_copy(d, e, to).wait_send()

            else:
                y_copy(d, e, to).wait_send()

        def run():
            total = own[d, e]
            for step in (1, 2, 3):
                src = (y + step) % 4
                slot = ybuf.at[d, e, src]
                remote(slot, slot, y_ssem.at[d, e, 0], y_rsem.at[d, e, src], right).wait_recv()
                total = total + ybuf[d, e, src].astype(F32)
            for col in (0, 1):
                part = total[:, 128 * col : 128 * col + 128].astype(xsend.dtype)

                @pl.when(2 * e + col == x)
                def _():
                    xbuf[d, x] = part

                @pl.when(2 * e + col != x)
                def _():
                    xsend[d, e, col] = part
                    x_copy(d, e, col).start()

        guarded(d, e, run)

    def kept(d):
        zs = my_chunk(d)
        return ((zs // 2) % 4 == y) & (zs // 8 == lx)

    def finish(d):
        def run():
            zs = my_chunk(d)
            total = xbuf[d, x].astype(F32)
            for step in (1, 2, 3):
                src = (x + step) % 4
                slot = xbuf.at[d, src]
                remote(slot, slot, x_ssem.at[d, 0, 0], x_rsem.at[d, src], right).wait_recv()
                total = total + xbuf[d, src].astype(F32)

            @pl.when(kept(d))
            def _():
                fbuf[zs % 2, y % 2, lx] = total

            @pl.when(jnp.logical_not(kept(d)))
            def _():
                fsend[d] = total
                f_copy(d).start()

        guarded(d, h, run)

    def over(lo, hi, f):
        for edge in (0, 8):
            if lo <= edge < hi:
                f(edge)
        lo, hi = max(lo, 1), min(hi, 8)
        if hi == lo + 1:
            f(lo)
        elif hi > lo:

            @pl.loop(lo, hi)
            def _(d):
                f(d)

    def pass_on(t, u):
        for way in (0, 1):
            zs = (z + 16 - t) % 16 if way == 0 else (z + t) % 16
            ring(zs, u, way, t).wait_recv()
            if t < 7 or way == u // 2:
                ring(zs, u, way, t).start()
            hand(zs, u).start()

    def sent_on(t):
        for way in (0, 1) if 0 < t < 8 else (0,):
            zs = (z + 16 - t) % 16 if way == 0 else (z + t) % 16
            for u in range(4):
                hand(zs, u).wait_send()
                if t == 0:
                    ring(zs, u, 0, t).wait_send()
                    ring(zs, u, 1, t).wait_send()
                elif t < 7 or (t == 7 and way == u // 2):
                    ring(zs, u, way, t).wait_send()

    def joins(lo, hi, e):
        over(lo, hi, lambda d: join(d, e))

    def finishes(lo, hi, e):
        if e is not h:
            over(lo, hi, finish)

    scored, joined = [], []
    caught = 0
    not_h = 1 - h

    def settle(t):
        while scored and scored[0][0] + LAG_Y <= t:
            _, lo, hi, e = scored.pop(0)
            joins(lo, hi, e)
            joined.append((t, lo, hi, e))
        while joined and joined[0][0] + LAG_X <= t:
            finishes(*joined.pop(0)[1:])

    def mine(t, d):
        score(d, h, True)
        scored.append((t, d, d + 1, h))

    def theirs(t, lo, hi):
        over(lo, hi, lambda d: score(d, not_h, False))
        scored.append((t, lo, hi, not_h))

    for t in range(1, 8):
        pass_on(t, 0)
        if t == 1:
            local_train.wait()
        settle(t)
        pass_on(t, 1)
        mine(t, t - 1)
        pass_on(t, 2)
        pass_on(t, 3)
        if t >= 2:
            sent_on(t - 2)
        if t >= LATE:
            if t == LATE:
                for piece in (0, 1):
                    rows = pl.ds(EDGES[piece], EDGES[piece + 1] - EDGES[piece])
                    local = tbuf.at[1 - h, rows]
                    remote(local, local, train_ssem.at[0], train_rsem.at[piece], partner).wait_recv()
            top = min(caught + CATCH, t)
            theirs(t, caught, top)
            caught = top
    mine(8, 7)
    theirs(8, caught, 8)
    for u in range(4):
        ring((z + 8) % 16, u, 0, 0).wait_recv()
        hand((z + 8) % 16, u).start()
    settle(6 + LAG_Y)
    mine(9, 8)
    theirs(9, 8, 9)
    settle(7 + LAG_Y)
    settle(8 + LAG_Y)
    settle(9 + LAG_Y)
    settle(99)

    factor = 1.0 / math.sqrt(8 * 4096)
    for j in (0, 1):
        ahead = (2 * layer + j - z + 16) % 16
        edge = (ahead == 0) | (ahead == 8)
        group = jnp.where(edge, h, jnp.where(ahead > 8, 1, 0))
        for cs in (0, 1):
            for col in (0, 1):
                slot = fbuf.at[j, cs, col]

                @pl.when((2 * group + cs != y) | (col != lx))
                def _():
                    remote(slot, slot, f_ssem.at[0], f_rsem.at[j, cs, col], right).wait_recv()

                total = fbuf[j, cs, col] * factor
                for s in range(STEPS):
                    for hh in range(2):
                        to = 32 * j + 16 * hh + 8 * cs
                        row = 24 * hh + 8 * s
                        out_ref[s, to : to + 8, 128 * col : 128 * col + 128] = total[row : row + 8]

    for piece in (0, 1):
        train_copy(piece).wait_send()
    for u in (0, 1):
        xq(u).wait_send()
    for t in (6, 7, 8):
        sent_on(t)

    def sent(d):
        for e in (0, 1):

            def run():
                for col in (0, 1):

                    @pl.when(2 * e + col != x)
                    def _():
                        x_copy(d, e, col).wait_send()

            guarded(d, e, run)

        def last():
            @pl.when(jnp.logical_not(kept(d)))
            def _():
                f_copy(d).wait_send()

        guarded(d, h, last)

    over(0, 9, sent)


def body(train_grads, query_grads, out_basis, in_basis, eigenvalues, block_order):
    train = train_grads.reshape(256, 4096)
    query = query_grads.reshape(4, 8, 4096)
    dma = pltpu.SemaphoreType.DMA
    return pl.pallas_call(
        kernel,
        out_shape=jax.ShapeDtypeStruct((STEPS, 64, 256), F32),
        in_specs=[pl.BlockSpec(memory_space=pltpu.HBM)] * 6,
        out_specs=pl.BlockSpec(memory_space=pltpu.VMEM),
        scratch_shapes=[
            pltpu.SMEM((4,), jnp.int32),
            pltpu.VMEM((4, 8, 4096), BF16),
            pltpu.VMEM((1, 64, 64), F32),
            pltpu.VMEM((1, 64, 64), F32),
            pltpu.VMEM((1, 4096), F32),
            dma((5,)),
            pltpu.VMEM((2, 256, 2048), BF16),
            pltpu.VMEM((16, 2, 2, 48, 1024), BF16),
            pltpu.VMEM((3, 2, 128, 128), F32),
            pltpu.VMEM((48, 1024), BF16),
            pltpu.VMEM((9, 2, 48, 256), F32),
            pltpu.VMEM((9, 2, 4, 48, 256), BF16),
            pltpu.VMEM((9, 2, 4, 48, 256), BF16),
            pltpu.VMEM((9, 2, 2, 48, 128), F32),
            pltpu.VMEM((9, 4, 48, 128), F32),
            pltpu.VMEM((9, 48, 128), F32),
            pltpu.VMEM((2, 2, 2, 48, 128), F32),
            dma, dma((2,)), dma((2,)), dma((2,)), dma((2,)),
            dma((2, 8, 4)), dma((16, 4)), dma((16, 4)), dma((16, 4)),
            dma((9, 2, 4)), dma((9, 2, 4)), dma((9, 2, 2)), dma((9, 4)), dma((9,)), dma((2, 2, 2)),
        ],
        compiler_params=pltpu.CompilerParams(
            collective_id=0, has_side_effects=True, vmem_limit_bytes=63 << 20
        ),
    )(block_order, train, query, out_basis, in_basis, eigenvalues)


def solution(mesh):
    placed = (
        P("dp", "layer", None),
        P(None, "dp", "layer", None),
        P("layer", None, None),
        P("layer", None, None),
        P("layer", None),
        P(),
    )
    return jax.shard_map(
        body, mesh=mesh, in_specs=placed, out_specs=P(None, "layer", "dp"), check_vma=False
    )
```

```python
import math

import jax
import jax.numpy as jnp
from jax import lax
from jax.experimental import pallas as pl
from jax.experimental.pallas import tpu as pltpu
from jax.sharding import PartitionSpec as P

STEPS = 3
MESH = pl.DeviceIdType.MESH
F32 = jnp.float32
BF16 = jnp.bfloat16
EDGES = (0, 32, 256)
LAG_Y = 2
LAG_X = 2
LATE = 5
CATCH = 3


def mm(a, b):
    return lax.dot_general(a, b, (((1,), (0,)), ((), ())), preferred_element_type=F32)


def split(x, parts):
    out = []
    for _ in range(parts):
        top = x.astype(BF16)
        out.append(top)
        x = x - top.astype(F32)
    return out


def mm3(x, y):
    return mm(x[0], y[0]) + (mm(x[0], y[1]) + mm(x[1], y[0]))


def twice(m):
    zero = jnp.zeros_like(m)
    return jnp.concatenate(
        [jnp.concatenate([m, zero], axis=1), jnp.concatenate([zero, m], axis=1)], axis=0
    )


def patterns():
    rows = lax.broadcasted_iota(jnp.int32, (512, 64), 0)
    cols = lax.broadcasted_iota(jnp.int32, (512, 64), 1)
    pick_row = ((rows >> 8) + 2 * ((rows & 255) >> 3) == cols).astype(F32).astype(BF16)
    k_rows = lax.broadcasted_iota(jnp.int32, (64, 512), 0)
    k_cols = lax.broadcasted_iota(jnp.int32, (64, 512), 1)
    pick_col = ((k_cols >> 8) + 2 * ((k_cols & 255) >> 3) == k_rows).astype(F32).astype(BF16)
    row_q = lax.broadcasted_iota(jnp.int32, (512, 512), 0) & 7
    col_q = lax.broadcasted_iota(jnp.int32, (512, 512), 1) & 7
    return pick_row, pick_col, row_q == col_q


def spread(m_parts, pick_row, pick_col, same):
    out = []
    for part in m_parts:
        tall = mm(pick_row, part).astype(BF16)
        full = mm(tall, pick_col)
        out.append(jnp.where(same, full, 0.0).astype(BF16))
    return out


def left_apply(kron_parts, blocks):
    lane = lax.broadcasted_iota(jnp.int32, (256, 128), 1)
    low = lane < 64

    def turn(v):
        return pltpu.roll(v, 64, 1)

    b0, b1, b2 = blocks
    even = jnp.concatenate([jnp.where(low, b0, turn(b1)), b2], axis=1)
    odd = jnp.concatenate([jnp.where(low, turn(b0), b1), turn(b2)], axis=1)
    right = jnp.concatenate([even, odd], axis=0)
    out = mm3(kron_parts, split(right, 2))
    top, bot = out[:256], out[256:]
    r0 = jnp.where(low, top[:, :128], turn(bot[:, :128]))
    r1 = jnp.where(low, turn(top[:, :128]), bot[:, :128])
    r2 = jnp.where(low, top[:, 128:], turn(bot[:, 128:]))
    return r0, r1, r2


def stack_groups(x, count):
    return jnp.concatenate([x[:, g * 128 : (g + 1) * 128] for g in range(count)], axis=0)


def unstack_groups(x, first, count):
    return jnp.concatenate([x[(first + g) * 8 : (first + g + 1) * 8] for g in range(count)], axis=1)


def kernel(
    order_hbm, train_ref, query_hbm, a_hbm, b_hbm, lam_hbm, out_ref,
    order_ref, query_ref, a_ref, b_ref, lam_ref, in_sem, tbuf, qbuf, pf, xqs, own, ysend, ybuf, xsend, xbuf, fsend, fbuf,
    train_sem, train_ssem, train_rsem, xq_ssem, xq_rsem, zs_ssem, c_ssem, z_rsem, c_rsem, y_ssem, y_rsem, x_ssem, x_rsem, f_ssem, f_rsem,
):
    dp = lax.axis_index("dp")
    layer = lax.axis_index("layer")
    z, h, c = dp // 4, (dp // 2) % 2, dp % 2
    lx, y = layer // 4, layer % 4
    x = 2 * h + lx

    def at(zz, hh, cc, ll, yy):
        return (4 * zz + 2 * hh + cc, 4 * ll + yy)

    copies = [
        pltpu.make_async_copy(src, dst, in_sem.at[i])
        for i, (src, dst) in enumerate(
            [
                (a_hbm, a_ref), (b_hbm, b_ref), (query_hbm, query_ref),
                (order_hbm, order_ref), (lam_hbm, lam_ref),
            ]
        )
    ]
    for copy in copies:
        copy.start()

    def at_x(xx):
        return at(z, xx // 2, c, xx % 2, y)

    right, left = at((z + 1) % 16, h, c, lx, y), at((z + 15) % 16, h, c, lx, y)
    other_core = at(z, h, 1 - c, lx, y)
    partner = at(z, 1 - h, c, lx, y)

    barrier = pltpu.get_barrier_semaphore()
    everyone = [right, left, other_core]
    for step in (1, 2, 3):
        aside = (y + step) % 4
        everyone += [at(z, h, c, lx, aside), at(z, h, c, 1 - lx, aside), at_x((x + step) % 4)]
    for device in everyone:
        pl.semaphore_signal(barrier, inc=1, device_id=device, device_id_type=MESH)

    def remote(src, dst, ssem, rsem, device):
        return pltpu.make_async_remote_copy(
            src_ref=src, dst_ref=dst, send_sem=ssem, recv_sem=rsem, device_id=device, device_id_type=MESH
        )

    half = 2048
    local_train = pltpu.make_async_copy(
        train_ref.at[:, pl.ds(pl.multiple_of(h * half, half), half)], tbuf.at[h], train_sem
    )
    local_train.start()

    def train_copy(piece):
        rows = pl.ds(EDGES[piece], EDGES[piece + 1] - EDGES[piece])
        return remote(
            train_ref.at[rows, pl.ds(pl.multiple_of((1 - h) * half, half), half)],
            tbuf.at[h, rows], train_ssem.at[piece], train_rsem.at[piece], partner,
        )

    shapes = patterns()
    copies[0].wait()
    copies[1].wait()
    b_mat = b_ref[0]
    a_mat = a_ref[0]
    forth = split(twice(b_mat), 3)
    back = split(twice(b_mat.T), 2)
    a_parts = split(a_mat, 2)
    at_parts = split(a_mat.T, 2)
    kron_in = spread(at_parts, *shapes)
    kron_out = spread(a_parts, *shapes)
    for copy in copies[2:]:
        copy.wait()
    pl.semaphore_wait(barrier, len(everyone))
    train_copy(0).start()
    lam = lam_ref[...]
    lam_rows = jnp.concatenate(
        [jnp.broadcast_to(lam[:, g * 128 : (g + 1) * 128], (8, 128)) for g in range(32)], axis=0
    )
    first = []
    for s in range(STEPS):
        raw = stack_groups(query_ref[order_ref[s]].astype(F32), 32).astype(BF16)
        first.append(mm(raw, forth[0]) + (mm(raw, forth[1]) + mm(raw, forth[2])))
    rotated = left_apply(kron_in, first)
    scaled = [mm3(split(r / lam_rows, 2), back) for r in rotated]
    ready = left_apply(kron_out, scaled)
    for s in range(STEPS):
        pf[s, 0] = ready[s][:128]
        pf[s, 1] = ready[s][128:]


    def unit(zs, cc, u):
        hh = h if u < 2 else 1 - h
        return qbuf.at[zs, cc, hh, pl.ds(0, 32) if u % 2 == 0 else pl.ds(32, 16)]

    def ring(zs, u, way, t):
        slot = unit(zs, c, u)
        return remote(slot, slot, zs_ssem.at[way, t, u], z_rsem.at[zs, u], right if way == 0 else left)

    def hand(zs, u):
        slot = unit(zs, c, u)
        return remote(slot, slot, c_ssem.at[zs, u], c_rsem.at[zs, u], other_core)

    def handed(zs, u):
        slot = unit(zs, 1 - c, u)
        return remote(slot, slot, c_ssem.at[zs, u], c_rsem.at[zs, u], other_core)

    def xq(u):
        rows = pl.ds(0, 32) if u == 0 else pl.ds(32, 16)
        return remote(xqs.at[rows], qbuf.at[z, c, h, rows], xq_ssem.at[u], xq_rsem.at[u], partner)

    def xq_in(u):
        slot = unit(z, c, 2 + u)
        return remote(slot, slot, xq_ssem.at[u], xq_rsem.at[u], partner)

    def tall(part):
        return jnp.concatenate([unstack_groups(part, 0, 8), unstack_groups(part, 8, 8)], axis=0)

    def launch(u):
        ring(z, u, 0, 0).start()
        ring(z, u, 1, 0).start()
        hand(z, u).start()

    xqs[...] = jnp.concatenate([tall(pf[s, 1 - h]) for s in range(STEPS)], axis=0).astype(BF16)
    xq(0).start()
    xq(1).start()
    qbuf[z, c, h] = jnp.concatenate([tall(pf[s, h]) for s in range(STEPS)], axis=0).astype(BF16)
    launch(0)
    launch(1)
    train_copy(1).start()
    for u in (0, 1):
        xq_in(u).wait_recv()
        launch(2 + u)

    def lone(d):
        return isinstance(d, int) and d in (0, 8)

    def chunks(d):
        return [(z + d) % 16] if lone(d) else [(z + 16 - d) % 16, (z + d) % 16]

    def my_chunk(d):
        return (z + d) % 16 if lone(d) else (z + 16 + (1 - 2 * (y // 2)) * d) % 16

    def y_copy(d, e, to):
        return remote(
            ysend.at[d, e, to], ybuf.at[d, e, y], y_ssem.at[d, e, to], y_rsem.at[d, e, y],
            at(z, h, c, lx, to),
        )

    def wide(zs):
        rows = qbuf[zs].astype(F32).reshape(12, 16, 1024)
        low, high = rows[:, :8].reshape(96, 1024), rows[:, 8:].reshape(96, 1024)
        return jnp.concatenate([low, high], axis=1).astype(BF16)

    def score(d, e, fresh):
        held = chunks(d)
        if fresh:
            for zs in held:
                for u in range(4):
                    handed(zs, u).wait_recv()
        lhs = jnp.concatenate([wide(zs) for zs in held], axis=0)
        part = lax.dot_general(lhs, tbuf[e], (((1,), (1,)), ((), ())), preferred_element_type=F32)
        for piece in range(2 * len(held)):
            rows = part[48 * piece : 48 * piece + 48]
            to = 2 * e + piece if lone(d) else (2, 3, 0, 1)[piece]

            @pl.when(to == y)
            def _():
                own[d, e] = rows

            ysend[d, e, to] = rows.astype(BF16)
        for step in (1, 2, 3):
            to = (y + step) % 4
            if lone(d):

                @pl.when(to // 2 == e)
                def _():
                    y_copy(d, e, to).start()

            else:
                y_copy(d, e, to).start()

    def x_copy(d, e, col):
        return remote(
            xsend.at[d, e, col], xbuf.at[d, x], x_ssem.at[d, e, col], x_rsem.at[d, x], at_x(2 * e + col)
        )

    def f_copy(d):
        zs = my_chunk(d)
        return remote(
            fsend.at[d], fbuf.at[zs % 2, y % 2, lx], f_ssem.at[d], f_rsem.at[zs % 2, y % 2, lx],
            at(z, h, c, zs // 8, (zs // 2) % 4),
        )

    def guarded(d, e, f):
        if lone(d):
            pl.when(y // 2 == e)(f)
        else:
            f()

    def join(d, e):
        for step in (1, 2, 3):
            to = (y + step) % 4
            if lone(d):

                @pl.when(to // 2 == e)
                def _():
                    y_copy(d, e, to).wait_send()

            else:
                y_copy(d, e, to).wait_send()

        def run():
            total = own[d, e]
            for step in (1, 2, 3):
                src = (y + step) % 4
                slot = ybuf.at[d, e, src]
                remote(slot, slot, y_ssem.at[d, e, 0], y_rsem.at[d, e, src], right).wait_recv()
                total = total + ybuf[d, e, src].astype(F32)
            for col in (0, 1):
                part = total[:, 128 * col : 128 * col + 128].astype(xsend.dtype)

                @pl.when(2 * e + col == x)
                def _():
                    xbuf[d, x] = part

                @pl.when(2 * e + col != x)
                def _():
                    xsend[d, e, col] = part
                    x_copy(d, e, col).start()

        guarded(d, e, run)

    def kept(d):
        zs = my_chunk(d)
        return ((zs // 2) % 4 == y) & (zs // 8 == lx)

    def finish(d):
        def run():
            zs = my_chunk(d)
            total = xbuf[d, x].astype(F32)
            for step in (1, 2, 3):
                src = (x + step) % 4
                slot = xbuf.at[d, src]
                remote(slot, slot, x_ssem.at[d, 0, 0], x_rsem.at[d, src], right).wait_recv()
                total = total + xbuf[d, src].astype(F32)

            @pl.when(kept(d))
            def _():
                fbuf[zs % 2, y % 2, lx] = total

            @pl.when(jnp.logical_not(kept(d)))
            def _():
                fsend[d] = total
                f_copy(d).start()

        guarded(d, h, run)

    def over(lo, hi, f):
        for edge in (0, 8):
            if lo <= edge < hi:
                f(edge)
        lo, hi = max(lo, 1), min(hi, 8)
        if hi == lo + 1:
            f(lo)
        elif hi > lo:

            @pl.loop(lo, hi)
            def _(d):
                f(d)

    def pass_on(t, u):
        for way in (0, 1):
            zs = (z + 16 - t) % 16 if way == 0 else (z + t) % 16
            ring(zs, u, way, t).wait_recv()
            if t < 7 or way == u // 2:
                ring(zs, u, way, t).start()
            hand(zs, u).start()

    def sent_on(t):
        for way in (0, 1) if 0 < t < 8 else (0,):
            zs = (z + 16 - t) % 16 if way == 0 else (z + t) % 16
            for u in range(4):
                hand(zs, u).wait_send()
                if t == 0:
                    ring(zs, u, 0, t).wait_send()
                    ring(zs, u, 1, t).wait_send()
                elif t < 7 or (t == 7 and way == u // 2):
                    ring(zs, u, way, t).wait_send()

    def joins(lo, hi, e):
        over(lo, hi, lambda d: join(d, e))

    def finishes(lo, hi, e):
        if e is not h:
            over(lo, hi, finish)

    scored, joined = [], []
    caught = 0
    not_h = 1 - h

    def settle(t):
        while scored and scored[0][0] + LAG_Y <= t:
            _, lo, hi, e = scored.pop(0)
            joins(lo, hi, e)
            joined.append((t, lo, hi, e))
        while joined and joined[0][0] + LAG_X <= t:
            finishes(*joined.pop(0)[1:])

    def mine(t, d):
        score(d, h, True)
        scored.append((t, d, d + 1, h))

    def theirs(t, lo, hi):
        over(lo, hi, lambda d: score(d, not_h, False))
        scored.append((t, lo, hi, not_h))

    for t in range(1, 8):
        pass_on(t, 0)
        if t == 1:
            local_train.wait()
        settle(t)
        pass_on(t, 1)
        mine(t, t - 1)
        pass_on(t, 2)
        pass_on(t, 3)
        if t >= 2:
            sent_on(t - 2)
        if t >= LATE:
            if t == LATE:
                for piece in (0, 1):
                    rows = pl.ds(EDGES[piece], EDGES[piece + 1] - EDGES[piece])
                    local = tbuf.at[1 - h, rows]
                    remote(local, local, train_ssem.at[0], train_rsem.at[piece], partner).wait_recv()
            top = min(caught + CATCH, t)
            theirs(t, caught, top)
            caught = top
    mine(8, 7)
    theirs(8, caught, 8)
    for u in range(4):
        ring((z + 8) % 16, u, 0, 0).wait_recv()
        hand((z + 8) % 16, u).start()
    settle(6 + LAG_Y)
    mine(9, 8)
    theirs(9, 8, 9)
    settle(9 + LAG_Y)
    settle(99)

    factor = 1.0 / math.sqrt(8 * 4096)
    for j in (0, 1):
        ahead = (2 * layer + j - z + 16) % 16
        edge = (ahead == 0) | (ahead == 8)
        group = jnp.where(edge, h, jnp.where(ahead > 8, 1, 0))
        for cs in (0, 1):
            for col in (0, 1):
                slot = fbuf.at[j, cs, col]

                @pl.when((2 * group + cs != y) | (col != lx))
                def _():
                    remote(slot, slot, f_ssem.at[0], f_rsem.at[j, cs, col], right).wait_recv()

                total = fbuf[j, cs, col] * factor
                for s in range(STEPS):
                    for hh in range(2):
                        to = 32 * j + 16 * hh + 8 * cs
                        row = 24 * hh + 8 * s
                        out_ref[s, to : to + 8, 128 * col : 128 * col + 128] = total[row : row + 8]

    for piece in (0, 1):
        train_copy(piece).wait_send()
    for u in (0, 1):
        xq(u).wait_send()
    for t in (6, 7, 8):
        sent_on(t)

    def sent(d):
        for e in (0, 1):

            def run():
                for col in (0, 1):

                    @pl.when(2 * e + col != x)
                    def _():
                        x_copy(d, e, col).wait_send()

            guarded(d, e, run)

        def last():
            @pl.when(jnp.logical_not(kept(d)))
            def _():
                f_copy(d).wait_send()

        guarded(d, h, last)

    over(0, 9, sent)


def body(train_grads, query_grads, out_basis, in_basis, eigenvalues, block_order):
    train = train_grads.reshape(256, 4096)
    query = query_grads.reshape(4, 8, 4096)
    dma = pltpu.SemaphoreType.DMA
    return pl.pallas_call(
        kernel,
        out_shape=jax.ShapeDtypeStruct((STEPS, 64, 256), F32),
        in_specs=[pl.BlockSpec(memory_space=pltpu.HBM)] * 6,
        out_specs=pl.BlockSpec(memory_space=pltpu.VMEM),
        scratch_shapes=[
            pltpu.SMEM((4,), jnp.int32),
            pltpu.VMEM((4, 8, 4096), BF16),
            pltpu.VMEM((1, 64, 64), F32),
            pltpu.VMEM((1, 64, 64), F32),
            pltpu.VMEM((1, 4096), F32),
            dma((5,)),
            pltpu.VMEM((2, 256, 2048), BF16),
            pltpu.VMEM((16, 2, 2, 48, 1024), BF16),
            pltpu.VMEM((3, 2, 128, 128), F32),
            pltpu.VMEM((48, 1024), BF16),
            pltpu.VMEM((9, 2, 48, 256), F32),
            pltpu.VMEM((9, 2, 4, 48, 256), BF16),
            pltpu.VMEM((9, 2, 4, 48, 256), BF16),
            pltpu.VMEM((9, 2, 2, 48, 128), BF16),
            pltpu.VMEM((9, 4, 48, 128), BF16),
            pltpu.VMEM((9, 48, 128), F32),
            pltpu.VMEM((2, 2, 2, 48, 128), F32),
            dma, dma((2,)), dma((2,)), dma((2,)), dma((2,)),
            dma((2, 8, 4)), dma((16, 4)), dma((16, 4)), dma((16, 4)),
            dma((9, 2, 4)), dma((9, 2, 4)), dma((9, 2, 2)), dma((9, 4)), dma((9,)), dma((2, 2, 2)),
        ],
        compiler_params=pltpu.CompilerParams(
            collective_id=0, has_side_effects=True, vmem_limit_bytes=63 << 20
        ),
    )(block_order, train, query, out_basis, in_basis, eigenvalues)


def solution(mesh):
    placed = (
        P("dp", "layer", None),
        P(None, "dp", "layer", None),
        P("layer", None, None),
        P("layer", None, None),
        P("layer", None),
        P(),
    )
    return jax.shard_map(
        body, mesh=mesh, in_specs=placed, out_specs=P(None, "layer", "dp"), check_vma=False
    )
```
